256 devices in a mesh: dp: 8 (over z), expert: 32 (over y, x, core).
Axes of the slice: x: 4, y: 4, z: 8, core: 2. Of those that a mesh axis runs over, the one named last changes fastest.
Arguments:
- tokens: bfloat16 [32768, 7168], P(('dp', 'expert')), may hold values from -6 to 6
- cotangent: bfloat16 [32768, 7168], P(('dp', 'expert')), may hold values from -6 to 6
- routes: int32 [32768, 8], P(('dp', 'expert')), may hold values from 0 to 255, as said below
- route_weights: bfloat16 [32768, 8], P(('dp', 'expert')), may hold values from 0.049804688 to 1
- weights: bfloat16 [7168, 3, 4096], P(None, None, 'expert'), may hold values from -0.1875 to 0.1875
Outputs:
- d_tokens: bfloat16 [32768, 7168], P(('dp', 'expert'))
- d_route_weights: float32 [32768, 8], P(('dp', 'expert'))
- d_weights: bfloat16 [7168, 3, 4096], P('dp', None, 'expert')
The draws below stay inside these ranges and needn't reach their ends.
Inputs may be any that keep to these rules, and one draw needn't show every extreme that they name: `routes`: each row names 8 different experts, at most one of them below 4. On the rows of one device each expert below 4 is named by 1 to 8 rows; in each data group one such expert is named by exactly 8 rows on every device of the group.
All inputs are finite; a program needn't handle non-finite values.
Results may differ from the reference program's by a relative error of at most 0.023.
Values may be sent and summed in bfloat16 or wider, within the bound.
No kernel may reach another device: no remote copies, remote signals or barrier semaphores. Data moves between devices by JAX's collectives and lax.ppermute only.
A program may use at most 128 MiB of HBM per device.

```python
import math
import jax
import jax.numpy as jnp
from jax import lax

D = 7168
ROUTED = 256
TOP = 8
ROWS = 128
H_DEV = 128
GROUP = 8
FF_WIN = 1024
E_WIN = 4
MOST = 8
TOKENS = 32768
N_DP = 8
N_EXPERT = 32


def shuffle_rows(subkey):
    return jax.random.permutation(subkey, ROWS)


def draw_routes(key, part):
    key = jax.random.fold_in(key, 7)
    blocks = N_DP * N_EXPERT
    subkeys = jax.random.split(key, 5)
    counts = jax.random.randint(subkeys[0], (blocks, E_WIN), 1, MOST + 1)
    fullest = jnp.repeat(jax.random.randint(subkeys[1], (N_DP,), 0, E_WIN), N_EXPERT)
    counts = jnp.where(jnp.arange(E_WIN)[None, :] == fullest[:, None], MOST, counts)
    bounds = jnp.cumsum(counts, axis=1)
    places = jax.vmap(shuffle_rows)(jax.random.split(subkeys[2], blocks))
    window_id = jnp.sum((places[:, :, None] >= bounds[:, None, :]).astype(jnp.int32), axis=2).reshape(TOKENS)
    scores = jax.random.randint(subkeys[3], (TOKENS, ROUTED - E_WIN), 0, 2 ** 20) * ROUTED + jnp.arange(ROUTED - E_WIN)[None, :]
    others = lax.top_k(scores, TOP)[1].astype(jnp.int32) + E_WIN
    win_slot = jax.random.randint(subkeys[4], (TOKENS, 1), 0, TOP)
    take_win = (jnp.arange(TOP)[None, :] == win_slot) & (window_id < E_WIN)[:, None]
    return jnp.where(take_win, window_id[:, None], others).astype(jnp.int32)


def levels(stream_key, dims, cuts, low, largest):
    gain = 1.0
    for axis_at, shards_of in cuts:
        heights = jax.random.uniform(jax.random.fold_in(jax.random.fold_in(stream_key, 6), axis_at), (shards_of,), jnp.float32, low / len(cuts), largest / len(cuts))
        gain = gain * jnp.repeat(jnp.exp(heights), dims[axis_at] // shards_of).reshape((-1,) + (1,) * (len(dims) - 1 - axis_at))
    return gain


def gaussian(stream_key, dims, scale, limit, cuts=(), kind=jnp.bfloat16):
    values = scale * jax.random.normal(stream_key, dims, jnp.float32)
    if cuts:
        values = values * levels(stream_key, dims, cuts, -0.22, 0.18)
    return jnp.clip(values, -limit, limit).astype(kind)


def setup_inputs(seed: int = 0) -> dict:
    streams_of = jax.random.split(jax.random.key(seed), 6)
    return {
        "tokens": gaussian(streams_of[0], (TOKENS, D), 1.0, 6.0, ((0, 256),)),
        "cotangent": gaussian(streams_of[1], (TOKENS, D), 1.0, 6.0, ((0, 256),)),
        "routes": draw_routes(jax.random.fold_in(streams_of[5], 71), 0),
        "route_weights": jnp.clip(jnp.exp(math.log(1.0) - 2.9996462 * jax.random.uniform(streams_of[3], (TOKENS, TOP), jnp.float32) ** levels(streams_of[3], (TOKENS, TOP), ((0, 256),), -0.2, 0.2)), 0.049804688, 1.0).astype(jnp.bfloat16),
        "weights": gaussian(streams_of[4], (D, 3, E_WIN * FF_WIN), FF_WIN ** -0.5, 0.1875, ((2, 32),)),
    }


def contract_rows(left, right):
    return lax.dot_general(left, right, (((0,), (0,)), ((), ())), preferred_element_type=jnp.float32)


def reference(tokens, cotangent, routes, route_weights, weights):
    rows_all, width = tokens.shape
    window = routes < E_WIN
    expert_row = jnp.sum(jnp.where(window, routes, 0), axis=1).astype(jnp.int32)
    has_row = jnp.any(window, axis=1)
    weight_row = jnp.sum(jnp.where(window, route_weights.astype(jnp.float32), 0.0), axis=1)
    capacity = N_DP * N_EXPERT * MOST
    d_tokens = jnp.zeros((rows_all, width), jnp.float32)
    d_row = jnp.zeros((rows_all,), jnp.float32)
    grad_blocks = []
    for expert_id in range(E_WIN):
        chosen = has_row & (expert_row == expert_id)
        picked = jnp.nonzero(chosen, size=capacity, fill_value=0)[0].astype(jnp.int32)
        live_rows = jnp.arange(capacity) < jnp.sum(chosen.astype(jnp.int32))
        x_rows = jnp.where(live_rows[:, None], tokens[picked], 0).astype(jnp.bfloat16)
        dy_rows = jnp.where(live_rows[:, None], cotangent[picked], 0).astype(jnp.bfloat16)
        w_rows = jnp.where(live_rows, weight_row[picked], 0.0)
        tokens_part = jnp.zeros((capacity, width), jnp.float32)
        weight_part = jnp.zeros((capacity,), jnp.float32)
        for shard_id in range(GROUP):
            column = (expert_id * GROUP + shard_id) * H_DEV
            weight_piece = weights[:, :, column:column + H_DEV]
            gate_val = jnp.dot(x_rows, weight_piece[:, 0, :], preferred_element_type=jnp.float32)
            up_val = jnp.dot(x_rows, weight_piece[:, 1, :], preferred_element_type=jnp.float32)
            sigmoid_g = jax.nn.sigmoid(gate_val)
            activation = gate_val * sigmoid_g
            hidden_act = (activation * up_val).astype(jnp.bfloat16)
            back_proj = jnp.dot(dy_rows, weight_piece[:, 2, :], preferred_element_type=jnp.float32)
            shard_weight = lax.optimization_barrier(jnp.sum(hidden_act.astype(jnp.float32) * back_proj, axis=1).astype(jnp.bfloat16))
            weight_part = weight_part + shard_weight.astype(jnp.float32)
            scaled = w_rows[:, None] * back_proj
            d_gate = (scaled * up_val * sigmoid_g * (1.0 + gate_val * (1.0 - sigmoid_g))).astype(jnp.bfloat16)
            d_up = (scaled * activation).astype(jnp.bfloat16)
            weighted = (w_rows[:, None] * hidden_act.astype(jnp.float32)).astype(jnp.bfloat16)
            shard_grad = jnp.dot(d_gate, weight_piece[:, 0, :].T, preferred_element_type=jnp.float32)
            shard_grad = shard_grad + jnp.dot(d_up, weight_piece[:, 1, :].T, preferred_element_type=jnp.float32)
            shard_grad = lax.optimization_barrier(shard_grad.astype(jnp.bfloat16))
            tokens_part = tokens_part + shard_grad.astype(jnp.float32)
            grad_blocks.append(jnp.stack([contract_rows(x_rows, d_gate), contract_rows(x_rows, d_up), contract_rows(dy_rows, weighted)], axis=1))
        d_tokens = d_tokens.at[picked].add(jnp.where(live_rows[:, None], tokens_part, 0.0))
        d_row = d_row.at[picked].add(jnp.where(live_rows, weight_part, 0.0))
    d_weights = jnp.concatenate(grad_blocks, axis=2).astype(jnp.bfloat16)
    d_route_weights = jnp.where(window, d_row[:, None], 0.0).astype(jnp.float32)
    return d_tokens.astype(jnp.bfloat16), d_route_weights, d_weights
```

```python
import functools
import jax
import jax.numpy as jnp
from jax import lax
from jax.experimental import pallas as pl
from jax.experimental.pallas import tpu as pltpu
from jax.sharding import PartitionSpec as P

GROUP = 8
MOST = 8
N_WIN = 4
NX = 4
NC = 2
SLOTS = N_WIN * MOST
LANES = 128
CHUNK = 1024
F32 = jnp.float32
BF16 = jnp.bfloat16
VMEM = pltpu.MemorySpace.VMEM
SMEM = pltpu.MemorySpace.SMEM


def shifted(dy, dx, dc):
    pairs = []
    for y in range(N_WIN):
        for x in range(NX):
            for c in range(NC):
                to = (((y + dy) % N_WIN) * NX + (x + dx) % NX) * NC + (c + dc) % NC
                pairs.append(((y * NX + x) * NC + c, to))
    return pairs


def send(array, dy=0, dx=0, dc=0):
    return lax.ppermute(array, "expert", shifted(dy, dx, dc))


def call(body, outs, operands, scalars=0, limit=40):
    specs = [pl.BlockSpec(memory_space=SMEM)] * scalars
    specs += [pl.BlockSpec(memory_space=VMEM)] * (len(operands) - scalars)
    return pl.pallas_call(
        body,
        out_shape=[jax.ShapeDtypeStruct(s, d) for s, d in outs],
        in_specs=specs,
        out_specs=[pl.BlockSpec(memory_space=VMEM)] * len(outs),
        compiler_params=pltpu.CompilerParams(vmem_limit_bytes=limit * 1024 * 1024),
    )(*operands)


def slots_of(y_ref, routes_ref):
    routes = routes_ref[...]
    rows = routes.shape[1]
    window = routes < N_WIN
    expert = jnp.sum(jnp.where(window, routes, 0), axis=0, keepdims=True)
    has = jnp.sum(jnp.where(window, 1, 0), axis=0, keepdims=True) > 0
    near = (expert + N_WIN - y_ref[0]) & (N_WIN - 1)
    member = (lax.broadcasted_iota(jnp.int32, (MOST, rows), 0) == near) & has
    upto = lax.broadcasted_iota(jnp.int32, (rows, rows), 0) <= lax.broadcasted_iota(
        jnp.int32, (rows, rows), 1
    )
    ones = jnp.where(member, 1.0, 0.0)
    rank = jnp.dot(
        ones.astype(BF16), jnp.where(upto, 1.0, 0.0).astype(BF16), preferred_element_type=F32
    )
    base = lax.broadcasted_iota(jnp.int32, (MOST, rows), 0).astype(F32) * MOST
    slot = jnp.sum(ones * (base + rank), axis=0, keepdims=True) - 1.0
    slot = jnp.where(has, slot, -1.0).astype(jnp.int32)
    return window, lax.broadcasted_iota(jnp.int32, (SLOTS, rows), 0) == slot


def pick_tokens(y_ref, routes_ref, rw_ref, tok_ref, *outs):
    window, select = slots_of(y_ref, routes_ref)
    weight = jnp.sum(jnp.where(window, rw_ref[...].astype(F32), 0.0), axis=0, keepdims=True)
    chosen = jnp.sum(jnp.where(select, weight, 0.0), axis=1, keepdims=True)
    rows = jnp.dot(
        jnp.where(select, 1.0, 0.0).astype(BF16), tok_ref[...], preferred_element_type=F32
    )
    width = rows.shape[1]
    lanes = jnp.broadcast_to(chosen, (SLOTS, LANES))
    for k, out in enumerate(outs):
        out[:, :width] = rows[k * MOST : (k + 1) * MOST].astype(BF16)
        out[:, width:] = lanes[k * MOST : (k + 1) * MOST].astype(BF16)


def pick_rows(y_ref, routes_ref, tok_ref, *outs):
    _, select = slots_of(y_ref, routes_ref)
    rows = jnp.dot(
        jnp.where(select, 1.0, 0.0).astype(BF16), tok_ref[...], preferred_element_type=F32
    )
    for k, out in enumerate(outs):
        out[...] = rows[k * MOST : (k + 1) * MOST].astype(BF16)


def rows_of(blocks, cols):
    return jnp.concatenate([b[:, cols] for b in blocks], axis=0)


def gate_up(n_blocks, *refs):
    blocks, w_ref, out = refs[:n_blocks], refs[n_blocks], refs[n_blocks + 1]
    width = w_ref.shape[1]
    total = None
    for at in range(0, width, CHUNK):
        cols = slice(at, at + CHUNK)
        both = jnp.concatenate([w_ref[0, cols, :], w_ref[1, cols, :]], axis=1)
        part = jnp.dot(rows_of(blocks, cols), both, preferred_element_type=F32)
        total = part if total is None else total + part
    out[...] = total


def backward(n_blocks, *refs):
    xs, dys = refs[:n_blocks], refs[n_blocks : 2 * n_blocks]
    gu_ref, w_ref, g_ref, sw_ref, dw_ref = refs[2 * n_blocks :]
    width, hidden = w_ref.shape[1:]
    back = None
    for at in range(0, width, CHUNK):
        cols = slice(at, at + CHUNK)
        part = jnp.dot(rows_of(dys, cols), w_ref[2, cols, :], preferred_element_type=F32)
        back = part if back is None else back + part
    gate, up = gu_ref[:, :hidden], gu_ref[:, hidden:]
    w = rows_of(xs, slice(width, width + LANES)).astype(F32)
    sig = jax.nn.sigmoid(gate)
    act = gate * sig
    hid = (act * up).astype(BF16).astype(F32)
    sw = jnp.sum(hid * back, axis=1, keepdims=True)
    sw_ref[...] = jnp.broadcast_to(sw, (sw.shape[0], LANES)).astype(BF16)
    scaled = w * back
    d_gate = (scaled * up * sig * (1.0 + gate * (1.0 - sig))).astype(BF16)
    d_up = (scaled * act).astype(BF16)
    weighted = (w * hid).astype(BF16)
    d_both = jnp.concatenate([d_gate, d_up], axis=1)
    g_ref[...] = d_both
    down = (((0,), (0,)), ((), ()))
    for at in range(0, width, CHUNK):
        cols = slice(at, at + CHUNK)
        d_in = lax.dot_general(rows_of(xs, cols), d_both, down, preferred_element_type=F32)
        d_out = lax.dot_general(rows_of(dys, cols), weighted, down, preferred_element_type=F32)
        dw_ref[0, cols, :] = d_in[:, :hidden].astype(BF16)
        dw_ref[1, cols, :] = d_in[:, hidden:].astype(BF16)
        dw_ref[2, cols, :] = d_out.astype(BF16)


def shard_grads(g_ref, sw_ref, w_ref, *outs):
    width = w_ref.shape[1]
    across = (((1,), (1,)), ((), ()))
    d_both = g_ref[...]
    for at in range(0, width, CHUNK):
        cols = slice(at, at + CHUNK)
        both = jnp.concatenate([w_ref[0, cols, :], w_ref[1, cols, :]], axis=1)
        grad = lax.dot_general(d_both, both, across, preferred_element_type=F32).astype(BF16)
        row = 0
        for out in outs:
            out[:, cols] = grad[row : row + out.shape[0]]
            row += out.shape[0]
    row = 0
    for out in outs:
        out[:, width:] = sw_ref[row : row + out.shape[0], :]
        row += out.shape[0]


def add_pairs(mine_ref, got_ref, *outs):
    row = 0
    for out in outs:
        rows = slice(row, row + out.shape[0])
        out[...] = (mine_ref[rows, :].astype(F32) + got_ref[rows, :].astype(F32)).astype(BF16)
        row += out.shape[0]


def add_all(a_ref, b_ref, c_ref, d_ref, *outs):
    for k, out in enumerate(outs):
        rows = slice(k * MOST, (k + 1) * MOST)
        total = (a_ref[rows, :].astype(F32) + b_ref[rows, :].astype(F32)) + (
            c_ref[rows, :].astype(F32) + d_ref[rows, :].astype(F32)
        )
        out[...] = total.astype(BF16)


def put_back(y_ref, routes_ref, b0, b1, b2, b3, dtok_ref, drw_ref):
    window, select = slots_of(y_ref, routes_ref)
    width = dtok_ref.shape[1]
    grads = jnp.concatenate([b[...].astype(F32) for b in (b0, b1, b2, b3)], axis=0)
    one = jnp.where(select, 1.0, 0.0)
    dtok_ref[...] = lax.dot_general(
        one.astype(BF16),
        grads[:, :width].astype(BF16),
        (((0,), (0,)), ((), ())),
        preferred_element_type=F32,
    ).astype(BF16)
    row = jnp.sum(one * grads[:, width : width + 1], axis=0, keepdims=True)
    drw_ref[...] = jnp.where(window, row, 0.0)


def local(tokens, cotangent, routes, route_weights, weights):
    width = tokens.shape[1]
    wide = width + LANES
    hidden = weights.shape[2]
    y = (lax.axis_index("expert") // (NX * NC)).astype(jnp.int32).reshape(1)
    routes_t = routes.T
    w_t = jnp.transpose(weights, (1, 0, 2))
    total = SLOTS * NX * NC

    x_out = call(pick_tokens, [((MOST, wide), BF16)] * N_WIN, [y, routes_t, route_weights.T, tokens], 1)
    x_mine = jnp.concatenate([x_out[0]] + [send(x_out[k], dy=k) for k in range(1, N_WIN)], axis=0)
    dy_out = call(pick_rows, [((MOST, width), BF16)] * N_WIN, [y, routes_t, cotangent], 1)
    dy_mine = jnp.concatenate([dy_out[0]] + [send(dy_out[k], dy=k) for k in range(1, N_WIN)], axis=0)

    def spread(mine):
        half = SLOTS // 2
        left, right = send(mine, dx=1), send(mine, dx=-1)
        far_a, far_b = send(left[:half], dx=1), send(right[half:], dx=-1)
        own = [mine, left, right, far_a, far_b]
        return own + [send(b, dc=1) for b in own]

    xs = spread(x_mine)
    gu = call(
        functools.partial(gate_up, len(xs)), [((total, 2 * hidden), F32)], [*xs, w_t]
    )[0]
    dys = spread(dy_mine)
    g, sw, dw = call(
        functools.partial(backward, len(xs)),
        [((total, 2 * hidden), BF16), ((total, LANES), BF16), ((3, width, hidden), BF16)],
        [*xs, *dys, gu, w_t],
    )
    d_weights = jnp.transpose(
        lax.psum_scatter(dw, "dp", scatter_dimension=1, tiled=True), (1, 0, 2)
    )
    mine, other = call(
        shard_grads, [((total // 2, wide), BF16)] * 2, [g, sw, w_t]
    )
    got = send(other, dc=1)
    parts = call(add_pairs, [((SLOTS, wide), BF16)] * NX, [mine, got])
    keep, to_left, to_right, to_far = parts
    back = call(
        add_all,
        [((MOST, wide), BF16)] * N_WIN,
        [keep, send(to_left, dx=-1), send(to_right, dx=1), send(to_far, dx=2)],
    )
    home = [back[0]] + [send(back[k], dy=-k) for k in range(1, N_WIN)]
    d_tokens, d_rw = call(
        put_back,
        [(tokens.shape, BF16), (routes_t.shape, F32)],
        [y, routes_t, *home],
        1,
    )
    return d_tokens, d_rw.T, d_weights


def solution(mesh):
    placed = (
        P(("dp", "expert"), None),
        P(("dp", "expert"), None),
        P(("dp", "expert"), None),
        P(("dp", "expert"), None),
        P(None, None, "expert"),
    )
    return jax.shard_map(
        local,
        mesh=mesh,
        in_specs=placed,
        out_specs=(P(("dp", "expert"), None), P(("dp", "expert"), None), P("dp", None, "expert")),
        check_vma=False,
    )
```

```python
import functools
import math

import jax
import jax.numpy as jnp
from jax import lax
from jax.experimental import pallas as pl
from jax.experimental.pallas import tpu as pltpu
from jax.sharding import PartitionSpec as P

GROUP = 8
MOST = 8
N_WIN = 4
NX = 4
NC = 2
SLOTS = N_WIN * MOST
LANES = 128
CHUNK = 1024
F32 = jnp.float32
BF16 = jnp.bfloat16
VMEM = pltpu.MemorySpace.VMEM
SMEM = pltpu.MemorySpace.SMEM


def shifted(dy, dx, dc):
    pairs = []
    for y in range(N_WIN):
        for x in range(NX):
            for c in range(NC):
                to = (((y + dy) % N_WIN) * NX + (x + dx) % NX) * NC + (c + dc) % NC
                pairs.append(((y * NX + x) * NC + c, to))
    return pairs


def send(array, dy=0, dx=0, dc=0):
    return lax.ppermute(array, "expert", shifted(dy, dx, dc))


def after(array, *others):
    return lax.optimization_barrier((array, *others))[0]


def call(body, outs, operands, scalars=0, flops=0, limit=12):
    moved = sum(o.size * o.dtype.itemsize for o in operands)
    moved += sum(math.prod(s) * jnp.dtype(d).itemsize for s, d in outs)
    specs = [pl.BlockSpec(memory_space=SMEM)] * scalars
    specs += [pl.BlockSpec(memory_space=VMEM)] * (len(operands) - scalars)
    return pl.pallas_call(
        body,
        out_shape=[jax.ShapeDtypeStruct(s, d) for s, d in outs],
        in_specs=specs,
        out_specs=[pl.BlockSpec(memory_space=VMEM)] * len(outs),
        cost_estimate=pl.CostEstimate(flops=flops, bytes_accessed=moved, transcendentals=0),
        compiler_params=pltpu.CompilerParams(vmem_limit_bytes=limit * 1024 * 1024),
    )(*operands)


def slots_of(y_ref, routes_ref):
    routes = routes_ref[...]
    rows = routes.shape[1]
    window = routes < N_WIN
    expert = jnp.sum(jnp.where(window, routes, 0), axis=0, keepdims=True)
    has = jnp.sum(jnp.where(window, 1, 0), axis=0, keepdims=True) > 0
    near = (expert + N_WIN - y_ref[0]) & (N_WIN - 1)
    member = (lax.broadcasted_iota(jnp.int32, (MOST, rows), 0) == near) & has
    upto = lax.broadcasted_iota(jnp.int32, (rows, rows), 0) <= lax.broadcasted_iota(
        jnp.int32, (rows, rows), 1
    )
    ones = jnp.where(member, 1.0, 0.0)
    rank = jnp.dot(
        ones.astype(BF16), jnp.where(upto, 1.0, 0.0).astype(BF16), preferred_element_type=F32
    )
    base = lax.broadcasted_iota(jnp.int32, (MOST, rows), 0).astype(F32) * MOST
    slot = jnp.sum(ones * (base + rank), axis=0, keepdims=True) - 1.0
    slot = jnp.where(has, slot, -1.0).astype(jnp.int32)
    return window, lax.broadcasted_iota(jnp.int32, (SLOTS, rows), 0) == slot


def pick_rows(y_ref, routes_ref, rw_ref, tok_ref, cot_ref, *outs):
    window, select = slots_of(y_ref, routes_ref)
    weight = jnp.sum(jnp.where(window, rw_ref[...].astype(F32), 0.0), axis=0, keepdims=True)
    chosen = jnp.sum(jnp.where(select, weight, 0.0), axis=1, keepdims=True)
    one = jnp.where(select, 1.0, 0.0).astype(BF16)
    rows_x = jnp.dot(one, tok_ref[...], preferred_element_type=F32)
    rows_dy = jnp.dot(one, cot_ref[...], preferred_element_type=F32)
    width = rows_x.shape[1]
    lanes = jnp.broadcast_to(chosen, (SLOTS, LANES))
    for k, out in enumerate(outs):
        at = slice(k * MOST, (k + 1) * MOST)
        out[:, :width] = rows_x[at].astype(BF16)
        out[:, width : width + LANES] = lanes[at].astype(BF16)
        out[:, width + LANES :] = rows_dy[at].astype(BF16)


def cut_columns(top_ref, bottom_ref, out):
    piece = out.shape[1]
    half = top_ref.shape[0]
    n_dp = out.shape[0] // (2 * SLOTS)
    for z in range(n_dp):
        for k, first in enumerate((z * piece, n_dp * piece + LANES + z * piece)):
            cols = slice(first, first + piece)
            at = (2 * z + k) * SLOTS
            out[at : at + half, :] = top_ref[:, cols]
            out[at + half : at + SLOTS, :] = bottom_ref[:, cols]


def join(*refs):
    for k, out in enumerate(refs[N_WIN:]):
        two = [b[...].astype(F32) for b in refs[2 * k : 2 * k + 2]]
        out[...] = jnp.concatenate(two, axis=0).astype(BF16)


def rows_of(blocks, cols):
    return jnp.concatenate([b[:, cols] for b in blocks], axis=0)


def side_by_side(w_refs, kinds, cols):
    return jnp.concatenate([w[k, cols, :] for w in w_refs for k in kinds], axis=1)


def experts(n_blocks, *refs):
    blocks, w_refs = refs[:n_blocks], refs[n_blocks : n_blocks + NC]
    g_ref, sw_ref = refs[n_blocks + NC :]
    width, hidden = w_refs[0].shape[1:]
    both, back = None, None
    for at in range(0, width, CHUNK):
        cols = slice(at, at + CHUNK)
        part = jnp.dot(
            rows_of(blocks, cols), side_by_side(w_refs, (0, 1), cols), preferred_element_type=F32
        )
        both = part if both is None else both + part
        rows_dy = rows_of(blocks, slice(width + LANES + at, width + LANES + at + CHUNK))
        part = jnp.dot(rows_dy, side_by_side(w_refs, (2,), cols), preferred_element_type=F32)
        back = part if back is None else back + part
    w = rows_of(blocks, slice(width, width + LANES)).astype(F32)
    sw = None
    grads = []
    for c in range(NC):
        gate = both[:, 2 * c * hidden : (2 * c + 1) * hidden]
        up = both[:, (2 * c + 1) * hidden : (2 * c + 2) * hidden]
        proj = back[:, c * hidden : (c + 1) * hidden]
        sig = jax.nn.sigmoid(gate)
        act = gate * sig
        hid = (act * up).astype(BF16).astype(F32)
        part = jnp.sum(hid * proj, axis=1, keepdims=True)
        sw = part if sw is None else sw + part
        scaled = w * proj
        grads.append((scaled * up * sig * (1.0 + gate * (1.0 - sig))).astype(BF16))
        grads.append((scaled * act).astype(BF16))
        g_ref[:, (2 * NC + c) * hidden : (2 * NC + c + 1) * hidden] = (w * hid).astype(BF16)
    g_ref[:, : 2 * NC * hidden] = jnp.concatenate(grads, axis=1)
    sw_ref[...] = jnp.broadcast_to(sw, (sw.shape[0], LANES)).astype(BF16)


def shard_grads(*refs):
    w_refs, (g_ref, sw_ref), outs = refs[:NC], refs[NC : NC + 2], refs[NC + 2 :]
    width, hidden = w_refs[0].shape[1:]
    d_both = g_ref[:, : 2 * NC * hidden]
    across = (((1,), (1,)), ((), ()))
    for at in range(0, width, CHUNK):
        cols = slice(at, at + CHUNK)
        grad = lax.dot_general(
            d_both, side_by_side(w_refs, (0, 1), cols), across, preferred_element_type=F32
        ).astype(BF16)
        for k, out in enumerate(outs):
            out[:, cols] = grad[k * SLOTS : (k + 1) * SLOTS]
    for k, out in enumerate(outs):
        out[:, width:] = sw_ref[k * SLOTS : (k + 1) * SLOTS, :]


def weight_grads(n_cuts, *refs):
    cuts, (g_ref, mine, other) = refs[:n_cuts], refs[n_cuts:]
    n_dp = g_ref.shape[0]
    hidden = mine.shape[2]
    blocks = [(cuts[0],), (cuts[1],), (cuts[2],), tuple(cuts[3:])]
    down = (((0,), (0,)), ((), ()))
    d_in, d_out = None, None
    for k, block in enumerate(blocks):
        pieces = []
        for ref in block:
            pieces += [ref[at : at + SLOTS, :] for at in range(0, ref.shape[0], SLOTS)]
        rows_x = jnp.concatenate(pieces[0::2], axis=0)
        rows_dy = jnp.concatenate(pieces[1::2], axis=0)
        at = slice(k * SLOTS, (k + 1) * SLOTS)
        grads = jnp.concatenate([g_ref[z, at, :] for z in range(n_dp)], axis=0)
        part_in = lax.dot_general(
            rows_x, grads[:, : 2 * NC * hidden], down, preferred_element_type=F32
        )
        part_out = lax.dot_general(
            rows_dy, grads[:, 2 * NC * hidden :], down, preferred_element_type=F32
        )
        d_in = part_in if d_in is None else d_in + part_in
        d_out = part_out if d_out is None else d_out + part_out
    mine[0] = d_in[:, :hidden]
    mine[1] = d_in[:, hidden : 2 * hidden]
    mine[2] = d_out[:, :hidden]
    other[0] = d_in[:, 2 * hidden : 3 * hidden].astype(BF16)
    other[1] = d_in[:, 3 * hidden :].astype(BF16)
    other[2] = d_out[:, hidden:].astype(BF16)


def add_cores(mine_ref, got_ref, out):
    out[...] = (mine_ref[...] + got_ref[...].astype(F32)).astype(BF16)


def add_all(a_ref, b_ref, c_ref, d_ref, *outs):
    for k, out in enumerate(outs):
        rows = slice(k * MOST, (k + 1) * MOST)
        total = (a_ref[rows, :].astype(F32) + b_ref[rows, :].astype(F32)) + (
            c_ref[rows, :].astype(F32) + d_ref[rows, :].astype(F32)
        )
        out[...] = total.astype(BF16)


def two_halves(left_ref, right_ref, _, *outs):
    half = outs[0].shape[0]
    outs[0][...] = left_ref[:half, :]
    outs[1][...] = right_ref[half:, :]


def put_back(y_ref, routes_ref, b0, b1, b2, b3, dtok_ref, drw_ref):
    window, select = slots_of(y_ref, routes_ref)
    width = dtok_ref.shape[1]
    grads = jnp.concatenate([b[...].astype(F32) for b in (b0, b1, b2, b3)], axis=0)
    one = jnp.where(select, 1.0, 0.0)
    dtok_ref[...] = lax.dot_general(
        one.astype(BF16),
        grads[:, :width].astype(BF16),
        (((0,), (0,)), ((), ())),
        preferred_element_type=F32,
    ).astype(BF16)
    row = jnp.sum(one * grads[:, width : width + 1], axis=0, keepdims=True)
    drw_ref[...] = jnp.where(window, row, 0.0)


def local(tokens, cotangent, routes, route_weights, weights):
    width = tokens.shape[1]
    wide = width + LANES
    hidden = weights.shape[2]
    y = (lax.axis_index("expert") // (NX * NC)).astype(jnp.int32).reshape(1)
    routes_t = routes.T
    w_t = jnp.transpose(weights, (1, 0, 2))
    total = SLOTS * NX

    n_dp = lax.axis_size("dp")
    piece = width // n_dp

    half = SLOTS // 2
    full = wide + width
    out = call(
        pick_rows,
        [((MOST, full), BF16)] * N_WIN,
        [y, routes_t, route_weights.T, tokens, cotangent],
        1,
    )
    got = [out[0]] + [send(out[k], dy=k) for k in range(1, N_WIN)]
    top, bottom = call(join, [((half, full), BF16)] * 2, got)
    left_top, right_bottom = send(top, dx=1), send(bottom, dx=-1)
    left_bottom, right_top = send(bottom, dx=1), send(top, dx=-1)
    far_top, far_bottom = send(left_top, dx=1), send(right_bottom, dx=-1)
    blocks = [top, bottom, left_top, left_bottom, right_top, right_bottom, far_top, far_bottom]
    cut = call(cut_columns, [((2 * n_dp * SLOTS, piece), BF16)], [top, bottom])[0]
    cut = lax.all_to_all(cut, "dp", split_axis=0, concat_axis=0, tiled=True)

    work = 2 * total * width * NC * hidden
    work = 2 * total * width * NC * hidden
    w_all = [w_t, send(w_t, dc=1)]
    g, sw = call(
        functools.partial(experts, len(blocks)),
        [((total, 3 * NC * hidden), BF16), ((total, LANES), BF16)],
        [*blocks, *w_all],
        flops=3 * work,
    )
    keep, to_left, to_right, to_far = call(
        shard_grads, [((SLOTS, wide), BF16)] * NX, [*w_all, g, sw], flops=2 * work
    )
    cut_left, cut_right = send(cut, dx=1), send(cut, dx=-1)
    to_left, to_right, to_far, cut_left, cut_right = lax.optimization_barrier(
        (to_left, to_right, to_far, cut_left, cut_right)
    )
    g_all = lax.all_gather(g, "dp", axis=0)
    back = call(
        add_all,
        [((MOST, wide), BF16)] * N_WIN,
        [keep, send(to_left, dx=-1), send(to_right, dx=1), send(to_far, dx=2)],
    )
    home = [back[0]] + [send(back[k], dy=-k) for k in range(1, N_WIN)]
    top, bottom = call(
        two_halves,
        [((n_dp * SLOTS, piece), BF16)] * 2,
        [cut_left, cut_right, back[0]],
    )
    cuts = [cut, cut_left, cut_right, send(top, dx=1), send(bottom, dx=-1)]
    g_all = after(g_all, *home[1:])
    d_tokens, d_rw = call(
        put_back,
        [(tokens.shape, BF16), (routes_t.shape, F32)],
        [y, routes_t, *home],
        1,
    )
    d_mine, d_other = call(
        functools.partial(weight_grads, len(cuts)),
        [((3, piece, hidden), F32), ((3, piece, hidden), BF16)],
        [*cuts, g_all],
        flops=3 * work,
    )
    d_weights = call(add_cores, [((3, piece, hidden), BF16)], [d_mine, send(d_other, dc=1)])[0]
    return d_tokens, d_rw.T, jnp.transpose(d_weights, (1, 0, 2))


def solution(mesh):
    placed = (
        P(("dp", "expert"), None),
        P(("dp", "expert"), None),
        P(("dp", "expert"), None),
        P(("dp", "expert"), None),
        P(None, None, "expert"),
    )
    return jax.shard_map(
        local,
        mesh=mesh,
        in_specs=placed,
        out_specs=(P(("dp", "expert"), None), P(("dp", "expert"), None), P("dp", None, "expert")),
        check_vma=False,
    )
```

```python
import functools
import math

import jax
import jax.numpy as jnp
from jax import lax
from jax.experimental import pallas as pl
from jax.experimental.pallas import tpu as pltpu
from jax.sharding import PartitionSpec as P

GROUP = 8
MOST = 8
N_WIN = 4
NX = 4
NC = 2
SLOTS = N_WIN * MOST
LANES = 128
CHUNK = 1024
F32 = jnp.float32
BF16 = jnp.bfloat16
VMEM = pltpu.MemorySpace.VMEM
SMEM = pltpu.MemorySpace.SMEM


def shifted(dy, dx, dc):
    pairs = []
    for y in range(N_WIN):
        for x in range(NX):
            for c in range(NC):
                to = (((y + dy) % N_WIN) * NX + (x + dx) % NX) * NC + (c + dc) % NC
                pairs.append(((y * NX + x) * NC + c, to))
    return pairs


def send(array, dy=0, dx=0, dc=0):
    return lax.ppermute(array, "expert", shifted(dy, dx, dc))


def after(array, *others):
    return lax.optimization_barrier((array, *others))[0]


def call(body, outs, operands, scalars=0, flops=0, limit=12):
    moved = sum(o.size * o.dtype.itemsize for o in operands)
    moved += sum(math.prod(s) * jnp.dtype(d).itemsize for s, d in outs)
    specs = [pl.BlockSpec(memory_space=SMEM)] * scalars
    specs += [pl.BlockSpec(memory_space=VMEM)] * (len(operands) - scalars)
    return pl.pallas_call(
        body,
        out_shape=[jax.ShapeDtypeStruct(s, d) for s, d in outs],
        in_specs=specs,
        out_specs=[pl.BlockSpec(memory_space=VMEM)] * len(outs),
        cost_estimate=pl.CostEstimate(flops=flops, bytes_accessed=moved, transcendentals=0),
        compiler_params=pltpu.CompilerParams(vmem_limit_bytes=limit * 1024 * 1024),
    )(*operands)


def slots_of(y_ref, routes_ref):
    routes = routes_ref[...]
    rows = routes.shape[1]
    window = routes < N_WIN
    expert = jnp.sum(jnp.where(window, routes, 0), axis=0, keepdims=True)
    has = jnp.sum(jnp.where(window, 1, 0), axis=0, keepdims=True) > 0
    near = (expert + N_WIN - y_ref[0]) & (N_WIN - 1)
    member = (lax.broadcasted_iota(jnp.int32, (MOST, rows), 0) == near) & has
    upto = lax.broadcasted_iota(jnp.int32, (rows, rows), 0) <= lax.broadcasted_iota(
        jnp.int32, (rows, rows), 1
    )
    ones = jnp.where(member, 1.0, 0.0)
    rank = jnp.dot(
        ones.astype(BF16), jnp.where(upto, 1.0, 0.0).astype(BF16), preferred_element_type=F32
    )
    base = lax.broadcasted_iota(jnp.int32, (MOST, rows), 0).astype(F32) * MOST
    slot = jnp.sum(ones * (base + rank), axis=0, keepdims=True) - 1.0
    slot = jnp.where(has, slot, -1.0).astype(jnp.int32)
    return window, lax.broadcasted_iota(jnp.int32, (SLOTS, rows), 0) == slot


def pick_rows(y_ref, routes_ref, rw_ref, tok_ref, cot_ref, *outs):
    window, select = slots_of(y_ref, routes_ref)
    weight = jnp.sum(jnp.where(window, rw_ref[...].astype(F32), 0.0), axis=0, keepdims=True)
    chosen = jnp.sum(jnp.where(select, weight, 0.0), axis=1, keepdims=True)
    one = jnp.where(select, 1.0, 0.0).astype(BF16)
    rows_x = jnp.dot(one, tok_ref[...], preferred_element_type=F32)
    rows_dy = jnp.dot(one, cot_ref[...], preferred_element_type=F32)
    width = rows_x.shape[1]
    lanes = jnp.broadcast_to(chosen, (SLOTS, LANES))
    for k, out in enumerate(outs):
        at = slice(k * MOST, (k + 1) * MOST)
        out[:, :width] = rows_x[at].astype(BF16)
        out[:, width : width + LANES] = lanes[at].astype(BF16)
        out[:, width + LANES :] = rows_dy[at].astype(BF16)


def cut_columns(top_ref, bottom_ref, out):
    piece = out.shape[1]
    half = top_ref.shape[0]
    n_dp = out.shape[0] // (2 * SLOTS)
    for z in range(n_dp):
        for k, first in enumerate((z * piece, n_dp * piece + LANES + z * piece)):
            cols = slice(first, first + piece)
            at = (2 * z + k) * SLOTS
            out[at : at + half, :] = top_ref[:, cols]
            out[at + half : at + SLOTS, :] = bottom_ref[:, cols]


def join(*refs):
    for k, out in enumerate(refs[N_WIN:]):
        two = [b[...].astype(F32) for b in refs[2 * k : 2 * k + 2]]
        out[...] = jnp.concatenate(two, axis=0).astype(BF16)


def rows_of(blocks, cols):
    return jnp.concatenate([b[:, cols] for b in blocks], axis=0)


def side_by_side(w_refs, kinds, cols):
    return jnp.concatenate([w[k, cols, :] for w in w_refs for k in kinds], axis=1)


def experts(n_blocks, *refs):
    blocks, w_refs = refs[:n_blocks], refs[n_blocks : n_blocks + NC]
    g_ref, sw_ref = refs[n_blocks + NC :]
    width, hidden = w_refs[0].shape[1:]
    both, back = None, None
    for at in range(0, width, CHUNK):
        cols = slice(at, at + CHUNK)
        part = jnp.dot(
            rows_of(blocks, cols), side_by_side(w_refs, (0, 1), cols), preferred_element_type=F32
        )
        both = part if both is None else both + part
        rows_dy = rows_of(blocks, slice(width + LANES + at, width + LANES + at + CHUNK))
        part = jnp.dot(rows_dy, side_by_side(w_refs, (2,), cols), preferred_element_type=F32)
        back = part if back is None else back + part
    w = rows_of(blocks, slice(width, width + LANES)).astype(F32)
    sw = None
    grads = []
    for c in range(NC):
        gate = both[:, 2 * c * hidden : (2 * c + 1) * hidden]
        up = both[:, (2 * c + 1) * hidden : (2 * c + 2) * hidden]
        proj = back[:, c * hidden : (c + 1) * hidden]
        sig = jax.nn.sigmoid(gate)
        act = gate * sig
        hid = (act * up).astype(BF16).astype(F32)
        part = jnp.sum(hid * proj, axis=1, keepdims=True)
        sw = part if sw is None else sw + part
        scaled = w * proj
        grads.append((scaled * up * sig * (1.0 + gate * (1.0 - sig))).astype(BF16))
        grads.append((scaled * act).astype(BF16))
        g_ref[:, (2 * NC + c) * hidden : (2 * NC + c + 1) * hidden] = (w * hid).astype(BF16)
    g_ref[:, : 2 * NC * hidden] = jnp.concatenate(grads, axis=1)
    sw_ref[...] = jnp.broadcast_to(sw, (sw.shape[0], LANES)).astype(BF16)


def shard_grads(*refs):
    w_refs, (g_ref, sw_ref), outs = refs[:NC], refs[NC : NC + 2], refs[NC + 2 :]
    width, hidden = w_refs[0].shape[1:]
    d_both = g_ref[:, : 2 * NC * hidden]
    across = (((1,), (1,)), ((), ()))
    for at in range(0, width, CHUNK):
        cols = slice(at, at + CHUNK)
        grad = lax.dot_general(
            d_both, side_by_side(w_refs, (0, 1), cols), across, preferred_element_type=F32
        ).astype(BF16)
        row = 0
        for out in outs:
            out[:, cols] = grad[row : row + out.shape[0]]
            row += out.shape[0]
    row = 0
    for out in outs:
        out[:, width:] = sw_ref[row : row + out.shape[0], :]
        row += out.shape[0]


def weight_grads(n_cuts, *refs):
    cuts, (g_ref, mine, other) = refs[:n_cuts], refs[n_cuts:]
    n_dp = g_ref.shape[0]
    hidden = mine.shape[2]
    blocks = [(cuts[0],), (cuts[1],), (cuts[2],), tuple(cuts[3:])]
    down = (((0,), (0,)), ((), ()))
    d_in, d_out = None, None
    for k, block in enumerate(blocks):
        pieces = []
        for ref in block:
            pieces += [ref[at : at + SLOTS, :] for at in range(0, ref.shape[0], SLOTS)]
        rows_x = jnp.concatenate(pieces[0::2], axis=0)
        rows_dy = jnp.concatenate(pieces[1::2], axis=0)
        at = slice(k * SLOTS, (k + 1) * SLOTS)
        grads = jnp.concatenate([g_ref[z, at, :] for z in range(n_dp)], axis=0)
        part_in = lax.dot_general(
            rows_x, grads[:, : 2 * NC * hidden], down, preferred_element_type=F32
        )
        part_out = lax.dot_general(
            rows_dy, grads[:, 2 * NC * hidden :], down, preferred_element_type=F32
        )
        d_in = part_in if d_in is None else d_in + part_in
        d_out = part_out if d_out is None else d_out + part_out
    mine[0] = d_in[:, :hidden]
    mine[1] = d_in[:, hidden : 2 * hidden]
    mine[2] = d_out[:, :hidden]
    other[0] = d_in[:, 2 * hidden : 3 * hidden].astype(BF16)
    other[1] = d_in[:, 3 * hidden :].astype(BF16)
    other[2] = d_out[:, hidden:].astype(BF16)


def add_cores(mine_ref, got_ref, out):
    out[...] = (mine_ref[...] + got_ref[...].astype(F32)).astype(BF16)


def add_far(left_ref, right_ref, top_ref, bottom_ref, left_out, right_out):
    half = top_ref.shape[0]
    left_out[:half, :] = (left_ref[:half, :].astype(F32) + top_ref[...].astype(F32)).astype(BF16)
    left_out[half:, :] = left_ref[half:, :]
    right_out[:half, :] = right_ref[:half, :]
    right_out[half:, :] = (
        right_ref[half:, :].astype(F32) + bottom_ref[...].astype(F32)
    ).astype(BF16)


def add_all(a_ref, b_ref, c_ref, *outs):
    for k, out in enumerate(outs):
        rows = slice(k * MOST, (k + 1) * MOST)
        total = a_ref[rows, :].astype(F32) + b_ref[rows, :].astype(F32)
        out[...] = (total + c_ref[rows, :].astype(F32)).astype(BF16)


def two_halves(left_ref, right_ref, _, *outs):
    half = outs[0].shape[0]
    outs[0][...] = left_ref[:half, :]
    outs[1][...] = right_ref[half:, :]


def put_back(y_ref, routes_ref, b0, b1, b2, b3, dtok_ref, drw_ref):
    window, select = slots_of(y_ref, routes_ref)
    width = dtok_ref.shape[1]
    grads = jnp.concatenate([b[...].astype(F32) for b in (b0, b1, b2, b3)], axis=0)
    one = jnp.where(select, 1.0, 0.0)
    dtok_ref[...] = lax.dot_general(
        one.astype(BF16),
        grads[:, :width].astype(BF16),
        (((0,), (0,)), ((), ())),
        preferred_element_type=F32,
    ).astype(BF16)
    row = jnp.sum(one * grads[:, width : width + 1], axis=0, keepdims=True)
    drw_ref[...] = jnp.where(window, row, 0.0)


def local(tokens, cotangent, routes, route_weights, weights):
    width = tokens.shape[1]
    wide = width + LANES
    hidden = weights.shape[2]
    y = (lax.axis_index("expert") // (NX * NC)).astype(jnp.int32).reshape(1)
    routes_t = routes.T
    w_t = jnp.transpose(weights, (1, 0, 2))
    total = SLOTS * NX

    n_dp = lax.axis_size("dp")
    piece = width // n_dp

    half = SLOTS // 2
    full = wide + width
    out = call(
        pick_rows,
        [((MOST, full), BF16)] * N_WIN,
        [y, routes_t, route_weights.T, tokens, cotangent],
        1,
    )
    got = [out[0]] + [send(out[k], dy=k) for k in range(1, N_WIN)]
    top, bottom = call(join, [((half, full), BF16)] * 2, got)
    left_top, right_bottom = send(top, dx=1), send(bottom, dx=-1)
    left_bottom, right_top = send(bottom, dx=1), send(top, dx=-1)
    far_top, far_bottom = send(left_top, dx=1), send(right_bottom, dx=-1)
    blocks = [top, bottom, left_top, left_bottom, right_top, right_bottom, far_top, far_bottom]
    cut = call(cut_columns, [((2 * n_dp * SLOTS, piece), BF16)], [top, bottom])[0]
    cut = lax.all_to_all(cut, "dp", split_axis=0, concat_axis=0, tiled=True)

    work = 2 * total * width * NC * hidden
    work = 2 * total * width * NC * hidden
    w_all = [w_t, send(w_t, dc=1)]
    g, sw = call(
        functools.partial(experts, len(blocks)),
        [((total, 3 * NC * hidden), BF16), ((total, LANES), BF16)],
        [*blocks, *w_all],
        flops=3 * work,
    )
    keep, to_left, to_right, far_up, far_down = call(
        shard_grads,
        [((SLOTS, wide), BF16)] * 3 + [((half, wide), BF16)] * 2,
        [*w_all, g, sw],
        flops=2 * work,
    )
    to_left, to_right = call(
        add_far,
        [((SLOTS, wide), BF16)] * 2,
        [to_left, to_right, send(far_up, dx=-1), send(far_down, dx=1)],
    )
    cut_left, cut_right = send(cut, dx=1), send(cut, dx=-1)
    to_left, to_right, cut_left, cut_right = lax.optimization_barrier(
        (to_left, to_right, cut_left, cut_right)
    )
    g_all = lax.all_gather(g, "dp", axis=0)
    back = call(
        add_all,
        [((MOST, wide), BF16)] * N_WIN,
        [keep, send(to_left, dx=-1), send(to_right, dx=1)],
    )
    home = [back[0]] + [send(back[k], dy=-k) for k in range(1, N_WIN)]
    top, bottom = call(
        two_halves,
        [((n_dp * SLOTS, piece), BF16)] * 2,
        [cut_left, cut_right, back[0]],
    )
    cuts = [cut, cut_left, cut_right, send(top, dx=1), send(bottom, dx=-1)]
    g_all = after(g_all, *home[1:])
    d_tokens, d_rw = call(
        put_back,
        [(tokens.shape, BF16), (routes_t.shape, F32)],
        [y, routes_t, *home],
        1,
    )
    d_mine, d_other = call(
        functools.partial(weight_grads, len(cuts)),
        [((3, piece, hidden), F32), ((3, piece, hidden), BF16)],
        [*cuts, g_all],
        flops=3 * work,
    )
    d_weights = call(add_cores, [((3, piece, hidden), BF16)], [d_mine, send(d_other, dc=1)])[0]
    return d_tokens, d_rw.T, jnp.transpose(d_weights, (1, 0, 2))


def solution(mesh):
    placed = (
        P(("dp", "expert"), None),
        P(("dp", "expert"), None),
        P(("dp", "expert"), None),
        P(("dp", "expert"), None),
        P(None, None, "expert"),
    )
    return jax.shard_map(
        local,
        mesh=mesh,
        in_specs=placed,
        out_specs=(P(("dp", "expert"), None), P(("dp", "expert"), None), P("dp", None, "expert")),
        check_vma=False,
    )
```

```python
import functools
import math

import jax
import jax.numpy as jnp
from jax import lax
from jax.experimental import pallas as pl
from jax.experimental.pallas import tpu as pltpu
from jax.sharding import PartitionSpec as P

GROUP = 8
MOST = 8
N_WIN = 4
NX = 4
NC = 2
SLOTS = N_WIN * MOST
LANES = 128
CHUNK = 1024
F32 = jnp.float32
BF16 = jnp.bfloat16
VMEM = pltpu.MemorySpace.VMEM
SMEM = pltpu.MemorySpace.SMEM


def shifted(dy, dx, dc):
    pairs = []
    for y in range(N_WIN):
        for x in range(NX):
            for c in range(NC):
                to = (((y + dy) % N_WIN) * NX + (x + dx) % NX) * NC + (c + dc) % NC
                pairs.append(((y * NX + x) * NC + c, to))
    return pairs


def send(array, dy=0, dx=0, dc=0):
    return lax.ppermute(array, "expert", shifted(dy, dx, dc))


def after(array, *others):
    return lax.optimization_barrier((array, *others))[0]


def call(body, outs, operands, scalars=0, flops=0, limit=12):
    moved = sum(o.size * o.dtype.itemsize for o in operands)
    moved += sum(math.prod(s) * jnp.dtype(d).itemsize for s, d in outs)
    specs = [pl.BlockSpec(memory_space=SMEM)] * scalars
    specs += [pl.BlockSpec(memory_space=VMEM)] * (len(operands) - scalars)
    return pl.pallas_call(
        body,
        out_shape=[jax.ShapeDtypeStruct(s, d) for s, d in outs],
        in_specs=specs,
        out_specs=[pl.BlockSpec(memory_space=VMEM)] * len(outs),
        cost_estimate=pl.CostEstimate(flops=flops, bytes_accessed=moved, transcendentals=0),
        compiler_params=pltpu.CompilerParams(vmem_limit_bytes=limit * 1024 * 1024),
    )(*operands)


def slots_of(y_ref, routes_ref):
    routes = routes_ref[...]
    rows = routes.shape[1]
    window = routes < N_WIN
    expert = jnp.sum(jnp.where(window, routes, 0), axis=0, keepdims=True)
    has = jnp.sum(jnp.where(window, 1, 0), axis=0, keepdims=True) > 0
    near = (expert + N_WIN - y_ref[0]) & (N_WIN - 1)
    member = (lax.broadcasted_iota(jnp.int32, (MOST, rows), 0) == near) & has
    upto = lax.broadcasted_iota(jnp.int32, (rows, rows), 0) <= lax.broadcasted_iota(
        jnp.int32, (rows, rows), 1
    )
    ones = jnp.where(member, 1.0, 0.0)
    rank = jnp.dot(
        ones.astype(BF16), jnp.where(upto, 1.0, 0.0).astype(BF16), preferred_element_type=F32
    )
    base = lax.broadcasted_iota(jnp.int32, (MOST, rows), 0).astype(F32) * MOST
    slot = jnp.sum(ones * (base + rank), axis=0, keepdims=True) - 1.0
    slot = jnp.where(has, slot, -1.0).astype(jnp.int32)
    return window, lax.broadcasted_iota(jnp.int32, (SLOTS, rows), 0) == slot


def pick_rows(y_ref, routes_ref, rw_ref, tok_ref, cot_ref, *outs):
    window, select = slots_of(y_ref, routes_ref)
    weight = jnp.sum(jnp.where(window, rw_ref[...].astype(F32), 0.0), axis=0, keepdims=True)
    chosen = jnp.sum(jnp.where(select, weight, 0.0), axis=1, keepdims=True)
    one = jnp.where(select, 1.0, 0.0).astype(BF16)
    rows_x = jnp.dot(one, tok_ref[...], preferred_element_type=F32)
    rows_dy = jnp.dot(one, cot_ref[...], preferred_element_type=F32)
    width = rows_x.shape[1]
    lanes = jnp.broadcast_to(chosen, (SLOTS, LANES))
    for k, out in enumerate(outs):
        at = slice(k * MOST, (k + 1) * MOST)
        out[:, :width] = rows_x[at].astype(BF16)
        out[:, width : width + LANES] = lanes[at].astype(BF16)
        out[:, width + LANES :] = rows_dy[at].astype(BF16)


def cut_columns(top_ref, bottom_ref, out):
    piece = out.shape[1]
    half = top_ref.shape[0]
    n_dp = out.shape[0] // (2 * SLOTS)
    for z in range(n_dp):
        for k, first in enumerate((z * piece, n_dp * piece + LANES + z * piece)):
            cols = slice(first, first + piece)
            at = (2 * z + k) * SLOTS
            out[at : at + half, :] = top_ref[:, cols]
            out[at + half : at + SLOTS, :] = bottom_ref[:, cols]


def join(*refs):
    for k, out in enumerate(refs[N_WIN:]):
        two = [b[...].astype(F32) for b in refs[2 * k : 2 * k + 2]]
        out[...] = jnp.concatenate(two, axis=0).astype(BF16)


def rows_of(blocks, cols):
    return jnp.concatenate([b[:, cols] for b in blocks], axis=0)


def side_by_side(w_refs, kinds, cols):
    return jnp.concatenate([w[k, cols, :] for w in w_refs for k in kinds], axis=1)


def experts(n_blocks, *refs):
    blocks, w_refs = refs[:n_blocks], refs[n_blocks : n_blocks + NC]
    g_ref, sw_ref = refs[n_blocks + NC :]
    width, hidden = w_refs[0].shape[1:]
    both, back = None, None
    for at in range(0, width, CHUNK):
        cols = slice(at, at + CHUNK)
        part = jnp.dot(
            rows_of(blocks, cols), side_by_side(w_refs, (0, 1), cols), preferred_element_type=F32
        )
        both = part if both is None else both + part
        rows_dy = rows_of(blocks, slice(width + LANES + at, width + LANES + at + CHUNK))
        part = jnp.dot(rows_dy, side_by_side(w_refs, (2,), cols), preferred_element_type=F32)
        back = part if back is None else back + part
    w = rows_of(blocks, slice(width, width + LANES)).astype(F32)
    sw = None
    grads = []
    for c in range(NC):
        gate = both[:, 2 * c * hidden : (2 * c + 1) * hidden]
        up = both[:, (2 * c + 1) * hidden : (2 * c + 2) * hidden]
        proj = back[:, c * hidden : (c + 1) * hidden]
        sig = jax.nn.sigmoid(gate)
        act = gate * sig
        hid = (act * up).astype(BF16).astype(F32)
        part = jnp.sum(hid * proj, axis=1, keepdims=True)
        sw = part if sw is None else sw + part
        scaled = w * proj
        grads.append((scaled * up * sig * (1.0 + gate * (1.0 - sig))).astype(BF16))
        grads.append((scaled * act).astype(BF16))
        g_ref[:, (2 * NC + c) * hidden : (2 * NC + c + 1) * hidden] = (w * hid).astype(BF16)
    g_ref[:, : 2 * NC * hidden] = jnp.concatenate(grads, axis=1)
    sw_ref[...] = jnp.broadcast_to(sw, (sw.shape[0], LANES)).astype(BF16)


def shard_grads(*refs):
    w_refs, (g_ref, sw_ref), outs = refs[:NC], refs[NC : NC + 2], refs[NC + 2 :]
    width, hidden = w_refs[0].shape[1:]
    d_both = g_ref[:, : 2 * NC * hidden]
    across = (((1,), (1,)), ((), ()))
    for at in range(0, width, CHUNK):
        cols = slice(at, at + CHUNK)
        grad = lax.dot_general(
            d_both, side_by_side(w_refs, (0, 1), cols), across, preferred_element_type=F32
        ).astype(BF16)
        row = 0
        for out in outs:
            out[:, cols] = grad[row : row + out.shape[0]]
            row += out.shape[0]
    row = 0
    for out in outs:
        out[:, width:] = sw_ref[row : row + out.shape[0], :]
        row += out.shape[0]


def weight_grads(n_cuts, *refs):
    cuts, (g_ref, mine, other) = refs[:n_cuts], refs[n_cuts:]
    n_dp = g_ref.shape[0]
    hidden = mine.shape[2]
    blocks = [(cuts[0],), (cuts[1],), (cuts[2],), tuple(cuts[3:])]
    down = (((0,), (0,)), ((), ()))
    d_in, d_out = None, None
    for k, block in enumerate(blocks):
        pieces = []
        for ref in block:
            pieces += [ref[at : at + SLOTS, :] for at in range(0, ref.shape[0], SLOTS)]
        rows_x = jnp.concatenate(pieces[0::2], axis=0)
        rows_dy = jnp.concatenate(pieces[1::2], axis=0)
        at = slice(k * SLOTS, (k + 1) * SLOTS)
        grads = jnp.concatenate([g_ref[z, at, :] for z in range(n_dp)], axis=0)
        part_in = lax.dot_general(
            rows_x, grads[:, : 2 * NC * hidden], down, preferred_element_type=F32
        )
        part_out = lax.dot_general(
            rows_dy, grads[:, 2 * NC * hidden :], down, preferred_element_type=F32
        )
        d_in = part_in if d_in is None else d_in + part_in
        d_out = part_out if d_out is None else d_out + part_out
    mine[0] = d_in[:, :hidden]
    mine[1] = d_in[:, hidden : 2 * hidden]
    mine[2] = d_out[:, :hidden]
    other[0] = d_in[:, 2 * hidden : 3 * hidden].astype(BF16)
    other[1] = d_in[:, 3 * hidden :].astype(BF16)
    other[2] = d_out[:, hidden:].astype(BF16)


def add_cores(mine_ref, got_ref, out):
    out[...] = (mine_ref[...] + got_ref[...].astype(F32)).astype(BF16)


def add_far(left_ref, right_ref, top_ref, bottom_ref, left_out, right_out):
    half = top_ref.shape[0]
    left_out[:half, :] = (left_ref[:half, :].astype(F32) + top_ref[...].astype(F32)).astype(BF16)
    left_out[half:, :] = left_ref[half:, :]
    right_out[:half, :] = right_ref[:half, :]
    right_out[half:, :] = (
        right_ref[half:, :].astype(F32) + bottom_ref[...].astype(F32)
    ).astype(BF16)


def add_all(a_ref, b_ref, c_ref, *outs):
    for k, out in enumerate(outs):
        rows = slice(k * MOST, (k + 1) * MOST)
        total = a_ref[rows, :].astype(F32) + b_ref[rows, :].astype(F32)
        out[...] = (total + c_ref[rows, :].astype(F32)).astype(BF16)


def two_halves(left_ref, right_ref, _, *outs):
    half = outs[0].shape[0]
    outs[0][...] = left_ref[:half, :]
    outs[1][...] = right_ref[half:, :]


def put_back(y_ref, routes_ref, b0, b1, b2, b3, dtok_ref, drw_ref):
    window, select = slots_of(y_ref, routes_ref)
    width = dtok_ref.shape[1]
    grads = jnp.concatenate([b[...].astype(F32) for b in (b0, b1, b2, b3)], axis=0)
    one = jnp.where(select, 1.0, 0.0)
    dtok_ref[...] = lax.dot_general(
        one.astype(BF16),
        grads[:, :width].astype(BF16),
        (((0,), (0,)), ((), ())),
        preferred_element_type=F32,
    ).astype(BF16)
    row = jnp.sum(one * grads[:, width : width + 1], axis=0, keepdims=True)
    drw_ref[...] = jnp.where(window, row, 0.0)


def local(tokens, cotangent, routes, route_weights, weights):
    width = tokens.shape[1]
    wide = width + LANES
    hidden = weights.shape[2]
    y = (lax.axis_index("expert") // (NX * NC)).astype(jnp.int32).reshape(1)
    routes_t = routes.T
    w_t = jnp.transpose(weights, (1, 0, 2))
    total = SLOTS * NX

    n_dp = lax.axis_size("dp")
    piece = width // n_dp

    half = SLOTS // 2
    full = wide + width
    out = call(
        pick_rows,
        [((MOST, full), BF16)] * N_WIN,
        [y, routes_t, route_weights.T, tokens, cotangent],
        1,
    )
    got = [out[0]] + [send(out[k], dy=k) for k in range(1, N_WIN)]
    top, bottom = call(join, [((half, full), BF16)] * 2, got)
    left_top, right_bottom = send(top, dx=1), send(bottom, dx=-1)
    left_bottom, right_top = send(bottom, dx=1), send(top, dx=-1)
    far_top, far_bottom = send(left_top, dx=1), send(right_bottom, dx=-1)
    blocks = [top, bottom, left_top, left_bottom, right_top, right_bottom, far_top, far_bottom]
    cut = call(cut_columns, [((2 * n_dp * SLOTS, piece), BF16)], [top, bottom])[0]
    cut = lax.all_to_all(cut, "dp", split_axis=0, concat_axis=0, tiled=True)

    work = 2 * total * width * NC * hidden
    work = 2 * total * width * NC * hidden
    w_all = [w_t, send(w_t, dc=1)]
    g, sw = call(
        functools.partial(experts, len(blocks)),
        [((total, 3 * NC * hidden), BF16), ((total, LANES), BF16)],
        [*blocks, *w_all],
        flops=6 * work,
    )
    keep, to_left, to_right, far_up, far_down = call(
        shard_grads,
        [((SLOTS, wide), BF16)] * 3 + [((half, wide), BF16)] * 2,
        [*w_all, g, sw],
        flops=2 * work,
    )
    to_left, to_right = call(
        add_far,
        [((SLOTS, wide), BF16)] * 2,
        [to_left, to_right, send(far_up, dx=-1), send(far_down, dx=1)],
    )
    cut_left, cut_right = send(cut, dx=1), send(cut, dx=-1)
    to_left, to_right, cut_left, cut_right = lax.optimization_barrier(
        (to_left, to_right, cut_left, cut_right)
    )
    g_all = lax.all_gather(g, "dp", axis=0)
    back = call(
        add_all,
        [((MOST, wide), BF16)] * N_WIN,
        [keep, send(to_left, dx=-1), send(to_right, dx=1)],
    )
    home = [back[0]] + [send(back[k], dy=-k) for k in range(1, N_WIN)]
    top, bottom = call(
        two_halves,
        [((n_dp * SLOTS, piece), BF16)] * 2,
        [cut_left, cut_right, back[0]],
    )
    cuts = [cut, cut_left, cut_right, send(top, dx=1), send(bottom, dx=-1)]
    g_all = after(g_all, *home[1:])
    d_tokens, d_rw = call(
        put_back,
        [(tokens.shape, BF16), (routes_t.shape, F32)],
        [y, routes_t, *home],
        1,
    )
    d_mine, d_other = call(
        functools.partial(weight_grads, len(cuts)),
        [((3, piece, hidden), F32), ((3, piece, hidden), BF16)],
        [*cuts, g_all],
        flops=3 * work,
    )
    d_weights = call(add_cores, [((3, piece, hidden), BF16)], [d_mine, send(d_other, dc=1)])[0]
    return d_tokens, d_rw.T, jnp.transpose(d_weights, (1, 0, 2))


def solution(mesh):
    placed = (
        P(("dp", "expert"), None),
        P(("dp", "expert"), None),
        P(("dp", "expert"), None),
        P(("dp", "expert"), None),
        P(None, None, "expert"),
    )
    return jax.shard_map(
        local,
        mesh=mesh,
        in_specs=placed,
        out_specs=(P(("dp", "expert"), None), P(("dp", "expert"), None), P("dp", None, "expert")),
        check_vma=False,
    )
```

```python
import functools
import math

import jax
import jax.numpy as jnp
from jax import lax
from jax.experimental import pallas as pl
from jax.experimental.pallas import tpu as pltpu
from jax.sharding import PartitionSpec as P

GROUP = 8
MOST = 8
N_WIN = 4
NX = 4
NC = 2
SLOTS = N_WIN * MOST
LANES = 128
CHUNK = 1024
F32 = jnp.float32
BF16 = jnp.bfloat16
VMEM = pltpu.MemorySpace.VMEM
SMEM = pltpu.MemorySpace.SMEM


def shifted(dy, dx, dc):
    pairs = []
    for y in range(N_WIN):
        for x in range(NX):
            for c in range(NC):
                to = (((y + dy) % N_WIN) * NX + (x + dx) % NX) * NC + (c + dc) % NC
                pairs.append(((y * NX + x) * NC + c, to))
    return pairs


def send(array, dy=0, dx=0, dc=0):
    return lax.ppermute(array, "expert", shifted(dy, dx, dc))


def after(array, *others):
    return lax.optimization_barrier((array, *others))[0]


def call(body, outs, operands, scalars=0, flops=0, limit=12, far=0, scratch=()):
    moved = sum(o.size * o.dtype.itemsize for o in operands)
    moved += sum(math.prod(s) * jnp.dtype(d).itemsize for s, d in outs)
    specs = [pl.BlockSpec(memory_space=SMEM)] * scalars
    specs += [pl.BlockSpec(memory_space=VMEM)] * (len(operands) - scalars - far)
    specs += [pl.BlockSpec(memory_space=pltpu.MemorySpace.HBM)] * far
    return pl.pallas_call(
        body,
        out_shape=[jax.ShapeDtypeStruct(s, d) for s, d in outs],
        in_specs=specs,
        out_specs=[pl.BlockSpec(memory_space=VMEM)] * len(outs),
        scratch_shapes=list(scratch),
        cost_estimate=pl.CostEstimate(flops=flops, bytes_accessed=moved, transcendentals=0),
        compiler_params=pltpu.CompilerParams(vmem_limit_bytes=limit * 1024 * 1024),
    )(*operands)


def slots_of(y_ref, routes_ref):
    routes = routes_ref[...]
    rows = routes.shape[1]
    window = routes < N_WIN
    expert = jnp.sum(jnp.where(window, routes, 0), axis=0, keepdims=True)
    has = jnp.sum(jnp.where(window, 1, 0), axis=0, keepdims=True) > 0
    near = (expert + N_WIN - y_ref[0]) & (N_WIN - 1)
    member = (lax.broadcasted_iota(jnp.int32, (MOST, rows), 0) == near) & has
    upto = lax.broadcasted_iota(jnp.int32, (rows, rows), 0) <= lax.broadcasted_iota(
        jnp.int32, (rows, rows), 1
    )
    ones = jnp.where(member, 1.0, 0.0)
    rank = jnp.dot(
        ones.astype(BF16), jnp.where(upto, 1.0, 0.0).astype(BF16), preferred_element_type=F32
    )
    base = lax.broadcasted_iota(jnp.int32, (MOST, rows), 0).astype(F32) * MOST
    slot = jnp.sum(ones * (base + rank), axis=0, keepdims=True) - 1.0
    slot = jnp.where(has, slot, -1.0).astype(jnp.int32)
    return window, lax.broadcasted_iota(jnp.int32, (SLOTS, rows), 0) == slot


def pick_rows(y_ref, routes_ref, rw_ref, tok_ref, cot_ref, *outs):
    window, select = slots_of(y_ref, routes_ref)
    weight = jnp.sum(jnp.where(window, rw_ref[...].astype(F32), 0.0), axis=0, keepdims=True)
    chosen = jnp.sum(jnp.where(select, weight, 0.0), axis=1, keepdims=True)
    one = jnp.where(select, 1.0, 0.0).astype(BF16)
    rows_x = jnp.dot(one, tok_ref[...], preferred_element_type=F32)
    rows_dy = jnp.dot(one, cot_ref[...], preferred_element_type=F32)
    width = rows_x.shape[1]
    lanes = jnp.broadcast_to(chosen, (SLOTS, LANES))
    for k, out in enumerate(outs):
        at = slice(k * MOST, (k + 1) * MOST)
        out[:, :width] = rows_x[at].astype(BF16)
        out[:, width : width + LANES] = lanes[at].astype(BF16)
        out[:, width + LANES :] = rows_dy[at].astype(BF16)


def cut_columns(top_ref, bottom_ref, out):
    piece = out.shape[1]
    half = top_ref.shape[0]
    n_dp = out.shape[0] // (2 * SLOTS)
    for z in range(n_dp):
        for k, first in enumerate((z * piece, n_dp * piece + LANES + z * piece)):
            cols = slice(first, first + piece)
            at = (2 * z + k) * SLOTS
            out[at : at + half, :] = top_ref[:, cols]
            out[at + half : at + SLOTS, :] = bottom_ref[:, cols]


def join(*refs):
    for k, out in enumerate(refs[N_WIN:]):
        two = [b[...].astype(F32) for b in refs[2 * k : 2 * k + 2]]
        out[...] = jnp.concatenate(two, axis=0).astype(BF16)


def rows_of(blocks, cols):
    return jnp.concatenate([b[:, cols] for b in blocks], axis=0)


def side_by_side(w_refs, kinds, cols):
    return jnp.concatenate([w[k, cols, :] for w in w_refs for k in kinds], axis=1)


def experts(n_blocks, *refs):
    blocks, w_far = refs[:n_blocks], refs[n_blocks : n_blocks + NC]
    g_ref, sw_ref, w_ref, sems = refs[n_blocks + NC :]
    width, hidden = w_far[0].shape[1:]
    copies = [
        [
            pltpu.make_async_copy(
                w_far[c].at[:, pl.ds(at, CHUNK), :],
                w_ref.at[c, :, pl.ds(at, CHUNK), :],
                sems.at[c, at // CHUNK],
            )
            for c in range(NC)
        ]
        for at in range(0, width, CHUNK)
    ]
    for two in copies:
        for copy in two:
            copy.start()
    w_refs = [w_ref.at[c] for c in range(NC)]
    both, back = None, None
    for at in range(0, width, CHUNK):
        cols = slice(at, at + CHUNK)
        for copy in copies[at // CHUNK]:
            copy.wait()
        part = jnp.dot(
            rows_of(blocks, cols), side_by_side(w_refs, (0, 1), cols), preferred_element_type=F32
        )
        both = part if both is None else both + part
        rows_dy = rows_of(blocks, slice(width + LANES + at, width + LANES + at + CHUNK))
        part = jnp.dot(rows_dy, side_by_side(w_refs, (2,), cols), preferred_element_type=F32)
        back = part if back is None else back + part
    w = rows_of(blocks, slice(width, width + LANES)).astype(F32)
    sw = None
    grads = []
    for c in range(NC):
        gate = both[:, 2 * c * hidden : (2 * c + 1) * hidden]
        up = both[:, (2 * c + 1) * hidden : (2 * c + 2) * hidden]
        proj = back[:, c * hidden : (c + 1) * hidden]
        sig = jax.nn.sigmoid(gate)
        act = gate * sig
        hid = (act * up).astype(BF16).astype(F32)
        part = jnp.sum(hid * proj, axis=1, keepdims=True)
        sw = part if sw is None else sw + part
        scaled = w * proj
        grads.append((scaled * up * sig * (1.0 + gate * (1.0 - sig))).astype(BF16))
        grads.append((scaled * act).astype(BF16))
        g_ref[:, (2 * NC + c) * hidden : (2 * NC + c + 1) * hidden] = (w * hid).astype(BF16)
    g_ref[:, : 2 * NC * hidden] = jnp.concatenate(grads, axis=1)
    sw_ref[...] = jnp.broadcast_to(sw, (sw.shape[0], LANES)).astype(BF16)


def shard_grads(*refs):
    w_refs, (g_ref, sw_ref), outs = refs[:NC], refs[NC : NC + 2], refs[NC + 2 :]
    width, hidden = w_refs[0].shape[1:]
    d_both = g_ref[:, : 2 * NC * hidden]
    across = (((1,), (1,)), ((), ()))
    for at in range(0, width, CHUNK):
        cols = slice(at, at + CHUNK)
        grad = lax.dot_general(
            d_both, side_by_side(w_refs, (0, 1), cols), across, preferred_element_type=F32
        ).astype(BF16)
        row = 0
        for out in outs:
            out[:, cols] = grad[row : row + out.shape[0]]
            row += out.shape[0]
    row = 0
    for out in outs:
        out[:, width:] = sw_ref[row : row + out.shape[0], :]
        row += out.shape[0]


def weight_grads(n_cuts, *refs):
    cuts, (g_ref, mine, other) = refs[:n_cuts], refs[n_cuts:]
    n_dp = g_ref.shape[0]
    hidden = mine.shape[2]
    blocks = [(cuts[0],), (cuts[1],), (cuts[2],), tuple(cuts[3:])]
    down = (((0,), (0,)), ((), ()))
    d_in, d_out = None, None
    for k, block in enumerate(blocks):
        pieces = []
        for ref in block:
            pieces += [ref[at : at + SLOTS, :] for at in range(0, ref.shape[0], SLOTS)]
        rows_x = jnp.concatenate(pieces[0::2], axis=0)
        rows_dy = jnp.concatenate(pieces[1::2], axis=0)
        at = slice(k * SLOTS, (k + 1) * SLOTS)
        grads = jnp.concatenate([g_ref[z, at, :] for z in range(n_dp)], axis=0)
        part_in = lax.dot_general(
            rows_x, grads[:, : 2 * NC * hidden], down, preferred_element_type=F32
        )
        part_out = lax.dot_general(
            rows_dy, grads[:, 2 * NC * hidden :], down, preferred_element_type=F32
        )
        d_in = part_in if d_in is None else d_in + part_in
        d_out = part_out if d_out is None else d_out + part_out
    mine[0] = d_in[:, :hidden]
    mine[1] = d_in[:, hidden : 2 * hidden]
    mine[2] = d_out[:, :hidden]
    other[0] = d_in[:, 2 * hidden : 3 * hidden].astype(BF16)
    other[1] = d_in[:, 3 * hidden :].astype(BF16)
    other[2] = d_out[:, hidden:].astype(BF16)


def add_cores(mine_ref, got_ref, out):
    out[...] = (mine_ref[...] + got_ref[...].astype(F32)).astype(BF16)


def add_far(left_ref, right_ref, top_ref, bottom_ref, left_out, right_out):
    half = top_ref.shape[0]
    left_out[:half, :] = (left_ref[:half, :].astype(F32) + top_ref[...].astype(F32)).astype(BF16)
    left_out[half:, :] = left_ref[half:, :]
    right_out[:half, :] = right_ref[:half, :]
    right_out[half:, :] = (
        right_ref[half:, :].astype(F32) + bottom_ref[...].astype(F32)
    ).astype(BF16)


def add_all(a_ref, b_ref, c_ref, *outs):
    for k, out in enumerate(outs):
        rows = slice(k * MOST, (k + 1) * MOST)
        total = a_ref[rows, :].astype(F32) + b_ref[rows, :].astype(F32)
        out[...] = (total + c_ref[rows, :].astype(F32)).astype(BF16)


def two_halves(left_ref, right_ref, _, *outs):
    half = outs[0].shape[0]
    outs[0][...] = left_ref[:half, :]
    outs[1][...] = right_ref[half:, :]


def put_back(y_ref, routes_ref, b0, b1, b2, b3, dtok_ref, drw_ref):
    window, select = slots_of(y_ref, routes_ref)
    width = dtok_ref.shape[1]
    grads = jnp.concatenate([b[...].astype(F32) for b in (b0, b1, b2, b3)], axis=0)
    one = jnp.where(select, 1.0, 0.0)
    dtok_ref[...] = lax.dot_general(
        one.astype(BF16),
        grads[:, :width].astype(BF16),
        (((0,), (0,)), ((), ())),
        preferred_element_type=F32,
    ).astype(BF16)
    row = jnp.sum(one * grads[:, width : width + 1], axis=0, keepdims=True)
    drw_ref[...] = jnp.where(window, row, 0.0)


def local(tokens, cotangent, routes, route_weights, weights):
    width = tokens.shape[1]
    wide = width + LANES
    hidden = weights.shape[2]
    y = (lax.axis_index("expert") // (NX * NC)).astype(jnp.int32).reshape(1)
    routes_t = routes.T
    w_t = jnp.transpose(weights, (1, 0, 2))
    total = SLOTS * NX

    n_dp = lax.axis_size("dp")
    piece = width // n_dp

    half = SLOTS // 2
    full = wide + width
    out = call(
        pick_rows,
        [((MOST, full), BF16)] * N_WIN,
        [y, routes_t, route_weights.T, tokens, cotangent],
        1,
    )
    got = [out[0]] + [send(out[k], dy=k) for k in range(1, N_WIN)]
    top, bottom = call(join, [((half, full), BF16)] * 2, got)
    left_top, right_bottom = send(top, dx=1), send(bottom, dx=-1)
    left_bottom, right_top = send(bottom, dx=1), send(top, dx=-1)
    far_top, far_bottom = send(left_top, dx=1), send(right_bottom, dx=-1)
    blocks = [top, bottom, left_top, left_bottom, right_top, right_bottom, far_top, far_bottom]
    cut = call(cut_columns, [((2 * n_dp * SLOTS, piece), BF16)], [top, bottom])[0]
    cut = lax.all_to_all(cut, "dp", split_axis=0, concat_axis=0, tiled=True)

    work = 2 * total * width * NC * hidden
    work = 2 * total * width * NC * hidden
    w_all = [w_t, send(w_t, dc=1)]
    g, sw = call(
        functools.partial(experts, len(blocks)),
        [((total, 3 * NC * hidden), BF16), ((total, LANES), BF16)],
        [*blocks, *w_all],
        flops=3 * work,
        limit=50,
        far=NC,
        scratch=[
            pltpu.VMEM((NC, 3, width, hidden), BF16),
            pltpu.SemaphoreType.DMA((NC, width // CHUNK)),
        ],
    )
    keep, to_left, to_right, far_up, far_down = call(
        shard_grads,
        [((SLOTS, wide), BF16)] * 3 + [((half, wide), BF16)] * 2,
        [*w_all, g, sw],
        flops=2 * work,
    )
    to_left, to_right = call(
        add_far,
        [((SLOTS, wide), BF16)] * 2,
        [to_left, to_right, send(far_up, dx=-1), send(far_down, dx=1)],
    )
    cut_left, cut_right = send(cut, dx=1), send(cut, dx=-1)
    to_left, to_right, cut_left, cut_right = lax.optimization_barrier(
        (to_left, to_right, cut_left, cut_right)
    )
    g_all = lax.all_gather(g, "dp", axis=0)
    back = call(
        add_all,
        [((MOST, wide), BF16)] * N_WIN,
        [keep, send(to_left, dx=-1), send(to_right, dx=1)],
    )
    home = [back[0]] + [send(back[k], dy=-k) for k in range(1, N_WIN)]
    top, bottom = call(
        two_halves,
        [((n_dp * SLOTS, piece), BF16)] * 2,
        [cut_left, cut_right, back[0]],
    )
    cuts = [cut, cut_left, cut_right, send(top, dx=1), send(bottom, dx=-1)]
    g_all = after(g_all, *home[1:])
    d_tokens, d_rw = call(
        put_back,
        [(tokens.shape, BF16), (routes_t.shape, F32)],
        [y, routes_t, *home],
        1,
    )
    d_mine, d_other = call(
        functools.partial(weight_grads, len(cuts)),
        [((3, piece, hidden), F32), ((3, piece, hidden), BF16)],
        [*cuts, g_all],
        flops=3 * work,
    )
    d_weights = call(add_cores, [((3, piece, hidden), BF16)], [d_mine, send(d_other, dc=1)])[0]
    return d_tokens, d_rw.T, jnp.transpose(d_weights, (1, 0, 2))


def solution(mesh):
    placed = (
        P(("dp", "expert"), None),
        P(("dp", "expert"), None),
        P(("dp", "expert"), None),
        P(("dp", "expert"), None),
        P(None, None, "expert"),
    )
    return jax.shard_map(
        local,
        mesh=mesh,
        in_specs=placed,
        out_specs=(P(("dp", "expert"), None), P(("dp", "expert"), None), P("dp", None, "expert")),
        check_vma=False,
    )
```

```python
import functools
import math

import jax
import jax.numpy as jnp
from jax import lax
from jax.experimental import pallas as pl
from jax.experimental.pallas import tpu as pltpu
from jax.sharding import PartitionSpec as P

GROUP = 8
MOST = 8
N_WIN = 4
NX = 4
NC = 2
SLOTS = N_WIN * MOST
LANES = 128
CHUNK = 1024
F32 = jnp.float32
BF16 = jnp.bfloat16
VMEM = pltpu.MemorySpace.VMEM
SMEM = pltpu.MemorySpace.SMEM


def shifted(dy, dx, dc):
    pairs = []
    for y in range(N_WIN):
        for x in range(NX):
            for c in range(NC):
                to = (((y + dy) % N_WIN) * NX + (x + dx) % NX) * NC + (c + dc) % NC
                pairs.append(((y * NX + x) * NC + c, to))
    return pairs


def send(array, dy=0, dx=0, dc=0):
    return lax.ppermute(array, "expert", shifted(dy, dx, dc))


def after(array, *others):
    return lax.optimization_barrier((array, *others))[0]


def call(body, outs, operands, scalars=0, flops=0, limit=12, far=0, scratch=()):
    moved = sum(o.size * o.dtype.itemsize for o in operands)
    moved += sum(math.prod(s) * jnp.dtype(d).itemsize for s, d in outs)
    specs = [pl.BlockSpec(memory_space=SMEM)] * scalars
    specs += [pl.BlockSpec(memory_space=VMEM)] * (len(operands) - scalars - far)
    specs += [pl.BlockSpec(memory_space=pltpu.MemorySpace.HBM)] * far
    return pl.pallas_call(
        body,
        out_shape=[jax.ShapeDtypeStruct(s, d) for s, d in outs],
        in_specs=specs,
        out_specs=[pl.BlockSpec(memory_space=VMEM)] * len(outs),
        scratch_shapes=list(scratch),
        cost_estimate=pl.CostEstimate(flops=flops, bytes_accessed=moved, transcendentals=0),
        compiler_params=pltpu.CompilerParams(vmem_limit_bytes=limit * 1024 * 1024),
    )(*operands)


def slots_of(y_ref, routes_ref):
    routes = routes_ref[...]
    rows = routes.shape[1]
    window = routes < N_WIN
    expert = jnp.sum(jnp.where(window, routes, 0), axis=0, keepdims=True)
    has = jnp.sum(jnp.where(window, 1, 0), axis=0, keepdims=True) > 0
    near = (expert + N_WIN - y_ref[0]) & (N_WIN - 1)
    member = (lax.broadcasted_iota(jnp.int32, (MOST, rows), 0) == near) & has
    upto = lax.broadcasted_iota(jnp.int32, (rows, rows), 0) <= lax.broadcasted_iota(
        jnp.int32, (rows, rows), 1
    )
    ones = jnp.where(member, 1.0, 0.0)
    rank = jnp.dot(
        ones.astype(BF16), jnp.where(upto, 1.0, 0.0).astype(BF16), preferred_element_type=F32
    )
    base = lax.broadcasted_iota(jnp.int32, (MOST, rows), 0).astype(F32) * MOST
    slot = jnp.sum(ones * (base + rank), axis=0, keepdims=True) - 1.0
    slot = jnp.where(has, slot, -1.0).astype(jnp.int32)
    return window, lax.broadcasted_iota(jnp.int32, (SLOTS, rows), 0) == slot


def pick_rows(y_ref, routes_ref, rw_ref, tok_ref, cot_ref, *outs):
    window, select = slots_of(y_ref, routes_ref)
    weight = jnp.sum(jnp.where(window, rw_ref[...].astype(F32), 0.0), axis=0, keepdims=True)
    chosen = jnp.sum(jnp.where(select, weight, 0.0), axis=1, keepdims=True)
    one = jnp.where(select, 1.0, 0.0).astype(BF16)
    rows_x = jnp.dot(one, tok_ref[...], preferred_element_type=F32)
    rows_dy = jnp.dot(one, cot_ref[...], preferred_element_type=F32)
    width = rows_x.shape[1]
    lanes = jnp.broadcast_to(chosen, (SLOTS, LANES))
    for k, out in enumerate(outs):
        at = slice(k * MOST, (k + 1) * MOST)
        out[:, :width] = rows_x[at].astype(BF16)
        out[:, width : width + LANES] = lanes[at].astype(BF16)
        out[:, width + LANES :] = rows_dy[at].astype(BF16)


def cut_columns(top_ref, bottom_ref, out):
    piece = out.shape[1]
    half = top_ref.shape[0]
    n_dp = out.shape[0] // (2 * SLOTS)
    for z in range(n_dp):
        for k, first in enumerate((z * piece, n_dp * piece + LANES + z * piece)):
            cols = slice(first, first + piece)
            at = (2 * z + k) * SLOTS
            out[at : at + half, :] = top_ref[:, cols]
            out[at + half : at + SLOTS, :] = bottom_ref[:, cols]


def join(*refs):
    for k, out in enumerate(refs[N_WIN:]):
        two = [b[...].astype(F32) for b in refs[2 * k : 2 * k + 2]]
        out[...] = jnp.concatenate(two, axis=0).astype(BF16)


def rows_of(blocks, cols):
    return jnp.concatenate([b[:, cols] for b in blocks], axis=0)


def side_by_side(w_refs, kinds, cols):
    return jnp.concatenate([w[k, cols, :] for w in w_refs for k in kinds], axis=1)


def experts(n_blocks, *refs):
    blocks, w_far = refs[:n_blocks], refs[n_blocks : n_blocks + NC]
    g_ref, sw_ref, w_ref, sems = refs[n_blocks + NC :]
    width, hidden = w_far[0].shape[1:]
    copies = [
        [
            pltpu.make_async_copy(
                w_far[c].at[:, pl.ds(at, CHUNK), :],
                w_ref.at[c, :, pl.ds(at, CHUNK), :],
                sems.at[c, at // CHUNK],
            )
            for c in range(NC)
        ]
        for at in range(0, width, CHUNK)
    ]
    for two in copies:
        for copy in two:
            copy.start()
    w_refs = [w_ref.at[c] for c in range(NC)]
    both, back = None, None
    for at in range(0, width, CHUNK):
        cols = slice(at, at + CHUNK)
        for copy in copies[at // CHUNK]:
            copy.wait()
        part = jnp.dot(
            rows_of(blocks, cols), side_by_side(w_refs, (0, 1), cols), preferred_element_type=F32
        )
        both = part if both is None else both + part
        rows_dy = rows_of(blocks, slice(width + LANES + at, width + LANES + at + CHUNK))
        part = jnp.dot(rows_dy, side_by_side(w_refs, (2,), cols), preferred_element_type=F32)
        back = part if back is None else back + part
    w = rows_of(blocks, slice(width, width + LANES)).astype(F32)
    sw = None
    grads = []
    for c in range(NC):
        gate = both[:, 2 * c * hidden : (2 * c + 1) * hidden]
        up = both[:, (2 * c + 1) * hidden : (2 * c + 2) * hidden]
        proj = back[:, c * hidden : (c + 1) * hidden]
        sig = jax.nn.sigmoid(gate)
        act = gate * sig
        hid = (act * up).astype(BF16).astype(F32)
        part = jnp.sum(hid * proj, axis=1, keepdims=True)
        sw = part if sw is None else sw + part
        scaled = w * proj
        grads.append((scaled * up * sig * (1.0 + gate * (1.0 - sig))).astype(BF16))
        grads.append((scaled * act).astype(BF16))
        g_ref[:, (2 * NC + c) * hidden : (2 * NC + c + 1) * hidden] = (w * hid).astype(BF16)
    g_ref[:, : 2 * NC * hidden] = jnp.concatenate(grads, axis=1)
    sw_ref[...] = jnp.broadcast_to(sw, (sw.shape[0], LANES)).astype(BF16)


def shard_grads(*refs):
    w_refs, (g_ref, sw_ref), outs = refs[:NC], refs[NC : NC + 2], refs[NC + 2 :]
    width, hidden = w_refs[0].shape[1:]
    d_both = g_ref[:, : 2 * NC * hidden]
    across = (((1,), (1,)), ((), ()))
    for at in range(0, width, CHUNK):
        cols = slice(at, at + CHUNK)
        grad = lax.dot_general(
            d_both, side_by_side(w_refs, (0, 1), cols), across, preferred_element_type=F32
        ).astype(BF16)
        row = 0
        for out in outs:
            out[:, cols] = grad[row : row + out.shape[0]]
            row += out.shape[0]
    row = 0
    for out in outs:
        out[:, width:] = sw_ref[row : row + out.shape[0], :]
        row += out.shape[0]


def weight_grads(n_cuts, *refs):
    cuts, (g_ref, mine, other) = refs[:n_cuts], refs[n_cuts:]
    n_dp = g_ref.shape[0]
    hidden = mine.shape[2]
    blocks = [(cuts[0],), (cuts[1],), (cuts[2],), tuple(cuts[3:])]
    down = (((0,), (0,)), ((), ()))
    d_in, d_out = None, None
    for k, block in enumerate(blocks):
        pieces = []
        for ref in block:
            pieces += [ref[at : at + SLOTS, :] for at in range(0, ref.shape[0], SLOTS)]
        rows_x = jnp.concatenate(pieces[0::2], axis=0)
        rows_dy = jnp.concatenate(pieces[1::2], axis=0)
        at = slice(k * SLOTS, (k + 1) * SLOTS)
        grads = jnp.concatenate([g_ref[z, at, :] for z in range(n_dp)], axis=0)
        part_in = lax.dot_general(
            rows_x, grads[:, : 2 * NC * hidden], down, preferred_element_type=F32
        )
        part_out = lax.dot_general(
            rows_dy, grads[:, 2 * NC * hidden :], down, preferred_element_type=F32
        )
        d_in = part_in if d_in is None else d_in + part_in
        d_out = part_out if d_out is None else d_out + part_out
    mine[0] = d_in[:, :hidden]
    mine[1] = d_in[:, hidden : 2 * hidden]
    mine[2] = d_out[:, :hidden]
    other[0] = d_in[:, 2 * hidden : 3 * hidden].astype(BF16)
    other[1] = d_in[:, 3 * hidden :].astype(BF16)
    other[2] = d_out[:, hidden:].astype(BF16)


def add_cores(mine_ref, got_ref, out):
    out[...] = (mine_ref[...] + got_ref[...].astype(F32)).astype(BF16)


def add_far(left_ref, right_ref, top_ref, bottom_ref, left_out, right_out):
    half = top_ref.shape[0]
    left_out[:half, :] = (left_ref[:half, :].astype(F32) + top_ref[...].astype(F32)).astype(BF16)
    left_out[half:, :] = left_ref[half:, :]
    right_out[:half, :] = right_ref[:half, :]
    right_out[half:, :] = (
        right_ref[half:, :].astype(F32) + bottom_ref[...].astype(F32)
    ).astype(BF16)


def add_all(a_ref, b_ref, c_ref, *outs):
    for k, out in enumerate(outs):
        rows = slice(k * MOST, (k + 1) * MOST)
        total = a_ref[rows, :].astype(F32) + b_ref[rows, :].astype(F32)
        out[...] = (total + c_ref[rows, :].astype(F32)).astype(BF16)


def two_halves(left_ref, right_ref, _, *outs):
    half = outs[0].shape[0]
    outs[0][...] = left_ref[:half, :]
    outs[1][...] = right_ref[half:, :]


def put_back(y_ref, routes_ref, b0, b1, b2, b3, dtok_ref, drw_ref):
    window, select = slots_of(y_ref, routes_ref)
    width = dtok_ref.shape[1]
    grads = jnp.concatenate([b[...].astype(F32) for b in (b0, b1, b2, b3)], axis=0)
    one = jnp.where(select, 1.0, 0.0)
    dtok_ref[...] = lax.dot_general(
        one.astype(BF16),
        grads[:, :width].astype(BF16),
        (((0,), (0,)), ((), ())),
        preferred_element_type=F32,
    ).astype(BF16)
    row = jnp.sum(one * grads[:, width : width + 1], axis=0, keepdims=True)
    drw_ref[...] = jnp.where(window, row, 0.0)


def local(tokens, cotangent, routes, route_weights, weights):
    width = tokens.shape[1]
    wide = width + LANES
    hidden = weights.shape[2]
    y = (lax.axis_index("expert") // (NX * NC)).astype(jnp.int32).reshape(1)
    routes_t = routes.T
    w_t = jnp.transpose(weights, (1, 0, 2))
    total = SLOTS * NX

    n_dp = lax.axis_size("dp")
    piece = width // n_dp

    half = SLOTS // 2
    full = wide + width
    out = call(
        pick_rows,
        [((MOST, full), BF16)] * N_WIN,
        [y, routes_t, route_weights.T, tokens, cotangent],
        1,
    )
    got = [out[0]] + [send(out[k], dy=k) for k in range(1, N_WIN)]
    top, bottom = call(join, [((half, full), BF16)] * 2, got)
    left_top, right_bottom = send(top, dx=1), send(bottom, dx=-1)
    left_bottom, right_top = send(bottom, dx=1), send(top, dx=-1)
    far_top, far_bottom = send(left_top, dx=1), send(right_bottom, dx=-1)
    blocks = [top, bottom, left_top, left_bottom, right_top, right_bottom, far_top, far_bottom]
    cut = call(cut_columns, [((2 * n_dp * SLOTS, piece), BF16)], [top, bottom])[0]
    cut = lax.all_to_all(cut, "dp", split_axis=0, concat_axis=0, tiled=True)

    work = 2 * total * width * NC * hidden
    work = 2 * total * width * NC * hidden
    w_all = [w_t, send(w_t, dc=1)]
    g, sw = call(
        functools.partial(experts, len(blocks)),
        [((total, 3 * NC * hidden), BF16), ((total, LANES), BF16)],
        [*blocks, *w_all],
        flops=3 * work,
        limit=50,
        far=NC,
        scratch=[
            pltpu.VMEM((NC, 3, width, hidden), BF16),
            pltpu.SemaphoreType.DMA((NC, width // CHUNK)),
        ],
    )
    keep, to_left, to_right, far_up, far_down = call(
        shard_grads,
        [((SLOTS, wide), BF16)] * 3 + [((half, wide), BF16)] * 2,
        [*w_all, g, sw],
        flops=2 * work,
    )
    to_left, to_right = call(
        add_far,
        [((SLOTS, wide), BF16)] * 2,
        [to_left, to_right, send(far_up, dx=-1), send(far_down, dx=1)],
    )
    cut_left, cut_right = send(cut, dx=1), send(cut, dx=-1)
    to_left, to_right, cut_left, cut_right = lax.optimization_barrier(
        (to_left, to_right, cut_left, cut_right)
    )
    g_all = lax.all_gather(g, "dp", axis=0)
    back = call(
        add_all,
        [((MOST, wide), BF16)] * N_WIN,
        [keep, send(to_left, dx=-1), send(to_right, dx=1)],
    )
    home = [back[0]] + [send(back[k], dy=-k) for k in range(1, N_WIN)]
    top, bottom = call(
        two_halves,
        [((n_dp * SLOTS, piece), BF16)] * 2,
        [cut_left, cut_right, back[0]],
    )
    cuts = [cut, cut_left, cut_right, send(top, dx=1), send(bottom, dx=-1)]
    g_all = after(g_all, *home[1:])
    d_tokens, d_rw = call(
        put_back,
        [(tokens.shape, BF16), (routes_t.shape, F32)],
        [y, routes_t, *home],
        1,
    )
    d_mine, d_other = call(
        functools.partial(weight_grads, len(cuts)),
        [((3, piece, hidden), F32), ((3, piece, hidden), BF16)],
        [*cuts, g_all],
        flops=3 * work,
        limit=52,
    )
    d_weights = call(add_cores, [((3, piece, hidden), BF16)], [d_mine, send(d_other, dc=1)])[0]
    return d_tokens, d_rw.T, jnp.transpose(d_weights, (1, 0, 2))


def solution(mesh):
    placed = (
        P(("dp", "expert"), None),
        P(("dp", "expert"), None),
        P(("dp", "expert"), None),
        P(("dp", "expert"), None),
        P(None, None, "expert"),
    )
    return jax.shard_map(
        local,
        mesh=mesh,
        in_specs=placed,
        out_specs=(P(("dp", "expert"), None), P(("dp", "expert"), None), P("dp", None, "expert")),
        check_vma=False,
    )
```
